512 devices in a mesh: pair: 128 (over y_hi, x, z), rep: 4 (over y_lo, core).
Axes of the slice: x: 4, y: 4 (y_hi: 2, y_lo: 2; y = y_hi * 2 + y_lo), z: 16, core: 2. Of those that a mesh axis runs over, the one named last changes fastest.
Arguments:
- amplitudes: bfloat16 [36864, 768], P('pair'), may hold values from -24 to 24
- lambda_amps: bfloat16 [36864, 4608], P('pair', 'rep'), may hold values from -6 to 6
- integrals: bfloat16 [768, 4608], P(None, 'rep'), may hold values from -0.21875 to 0.21875
- pair_map: int32 [384, 8], replicated, may hold values from 0 to 1, as said below
Outputs:
- ladder: bfloat16 [36864, 4608], P('pair', 'rep')
- lambda_ladder: bfloat16 [36864, 768], P('pair', 'rep')
- density: float32 [768, 4608], P('pair', 'rep')
The draws below stay inside these ranges and needn't reach their ends.
Inputs may be any that keep to these rules, and one draw needn't show every extreme that they name: `pair_map`: 1 marks a live block of an occupied-pair tile and a window virtual-pair tile, 0 an empty one.
All inputs are finite; a program needn't handle non-finite values.
Results may differ from the reference program's by a relative error of at most 0.013.
Values may be sent and summed in bfloat16 or wider, within the bound.
A program may use at most 64 MiB of HBM per device.

```python
import jax
import jax.numpy as jnp
from jax import lax

TW = 96
KT = 8
PAIRS = 36864
PTILES = 384
KW = 768
NAB = 4608
N_REP = 4


def draw_pair_map(key, part):
    key = jax.random.fold_in(key, 7)
    raw = jax.random.randint(key, (PTILES, KT), 0, 1000)
    row_index = jnp.arange(PTILES, dtype=jnp.int32)[:, None]
    limit = 250 + 500 * row_index // max(PTILES - 1, 1)
    return (raw < limit).astype(jnp.int32)


def spiked(values, rng, source, target, shards_of, factor):
    owner, partner = [(jnp.arange(values.shape[dim]) // (values.shape[dim] // shards_of)).reshape([-1 if axis == dim else 1 for axis in range(values.ndim)]) for dim in (source, target)]
    chosen = jax.random.permutation(rng, shards_of)[partner]
    strong = (owner == chosen) | (owner == (partner + shards_of // 2) % shards_of)
    return jnp.where(strong, factor * values, values)


def level_of(own_key, shape, cuts, low, top_value):
    level, own = 1.0, jax.random.fold_in(own_key, 6)
    for dim, blocks in cuts:
        heights = jnp.exp(jax.random.uniform(jax.random.fold_in(own, dim), (blocks,), jnp.float32, low / len(cuts), top_value / len(cuts)))
        level = level * jnp.repeat(heights, shape[dim] // blocks).reshape([-1 if axis == dim else 1 for axis in range(len(shape))])
    return level


def bell_draw(rng, shape, width, bound, cuts=(), kind=jnp.bfloat16):
    entries = width * jax.random.normal(rng, shape, jnp.float32)
    if cuts:
        entries = entries * level_of(rng, shape, cuts, -0.22, 0.18)
    return jnp.clip(entries, -bound, bound).astype(kind)


def gaussian_with(rng, extent, deviation, most, pieces, heavy, kind=jnp.bfloat16):
    entries = deviation * jax.random.normal(rng, extent, jnp.float32)
    if pieces:
        entries = entries * level_of(rng, extent, pieces, -0.22, 0.18)
    return jnp.clip(spiked(entries, jax.random.fold_in(rng, 3), *heavy), -most, most).astype(kind)


def setup_inputs(seed: int = 0) -> dict:
    key_list = jax.random.split(jax.random.key(seed), 5)
    amplitudes = gaussian_with(key_list[0], (PAIRS, KW), 1.0, 24.0, ((0, 128),), (0, 1, 128, 5.5))
    lambda_amps = bell_draw(key_list[1], (PAIRS, NAB), 1.0, 6.0, ((0, 128), (1, 4)))
    integrals = bell_draw(key_list[2], (KW, NAB), KW ** -0.5, 0.21875, ((1, 4),))
    pair_map = draw_pair_map(jax.random.fold_in(key_list[4], 71), 0)
    return dict(amplitudes=amplitudes, lambda_amps=lambda_amps, integrals=integrals, pair_map=pair_map)


def reference(amplitudes, lambda_amps, integrals, pair_map):
    live_mask = jnp.repeat(jnp.repeat(pair_map, TW, axis=0), TW, axis=1)
    mask_float = live_mask.astype(jnp.float32)
    amp_live = amplitudes * live_mask.astype(jnp.bfloat16)
    ladder = jnp.dot(amp_live, integrals, preferred_element_type=jnp.float32).astype(jnp.bfloat16)
    block_cols = NAB // N_REP
    total = jnp.zeros((PAIRS, KW), jnp.float32)
    for block in range(N_REP):
        lam_block = lambda_amps[:, block * block_cols:(block + 1) * block_cols]
        int_block = integrals[:, block * block_cols:(block + 1) * block_cols]
        partial_value = lax.dot_general(lam_block, int_block, (((1,), (1,)), ((), ())), preferred_element_type=jnp.float32)
        rounded = lax.optimization_barrier((partial_value * mask_float).astype(jnp.bfloat16))
        total = total + rounded.astype(jnp.float32)
    lambda_ladder = total.astype(jnp.bfloat16)
    factor = 1.0 / (PAIRS ** 0.5)
    density = lax.dot_general(amp_live, lambda_amps, (((0,), (0,)), ((), ())), preferred_element_type=jnp.float32) * factor
    return ladder, lambda_ladder, density
```

```python
import functools

import jax
import jax.numpy as jnp
from jax import lax
from jax.experimental import pallas as pl
from jax.experimental.pallas import tpu as pltpu
from jax.sharding import PartitionSpec as P

TW = 96
NY, NX, NZ = 2, 4, 16
NREP = 4
OWN = 6
PAD = 8
MESH = pl.DeviceIdType.MESH
PARTS = (
    (0, 384, "y,x"),
    (384, 256, "x,y"),
    (640, 256, "x,y"),
    (896, 256, "xy"),
)


def div3(value, shift):
    return ((value >> shift) * 21846) >> 16


def kernel(amp_h, lam_h, int_h, pm_h, lad_o, ll_o, den_o, *scratch):
    (amp, lam, ints, pmap, ampt, lad, lpart, lrecv, lsem, ssem, rsem), bufs = scratch[:11], scratch[11:]
    pidx, rep = lax.axis_index("pair"), lax.axis_index("rep")
    z, x, y = lax.rem(pidx, NZ), lax.rem(pidx // NZ, NX), pidx // (NZ * NX)
    loads = [
        pltpu.make_async_copy(src, dst, lsem.at[k])
        for k, (src, dst) in enumerate(((pm_h, pmap), (amp_h, amp), (lam_h, lam), (int_h, ints)))
    ]
    for load in loads:
        load.start()

    def at(yy, xx, zz):
        return ((yy * NX + xx) * NZ + zz, rep)

    def xs(d):
        return lax.rem(x + d, NX)

    def zs(d):
        return lax.rem(z + d, NZ)

    offsets = [(dy, dx) for dx in (2, 1, 3, 0) for dy in (1, 0) if (dy, dx) != (0, 0)]
    zorder = (8, 7, 9, 6, 10, 5, 11, 4, 12, 3, 13, 2, 14, 1, 15)
    partners = [at(lax.rem(y + dy, NY), xs(dx), z) for dy, dx in offsets]
    partners += [at(y, x, zs(d)) for d in zorder]
    partners += [(pidx, lax.rem(rep + d, NREP)) for d in (1, 2, 3)]
    barrier = pltpu.get_barrier_semaphore()
    for device in partners:
        pl.semaphore_signal(barrier, inc=1, device_id=device, device_id_type=MESH)

    count = [0]

    def send(src, dst, device):
        k = count[0]
        count[0] += 1
        copy = pltpu.make_async_remote_copy(
            src_ref=src, dst_ref=dst, send_sem=ssem.at[k], recv_sem=rsem.at[k],
            device_id=device, device_id_type=MESH,
        )
        copy.start()
        return copy

    rows = amp.shape[0]
    f32, bf16 = jnp.float32, jnp.bfloat16

    def iota(shape, dim):
        return lax.broadcasted_iota(jnp.int32, shape, dim)

    tiles = rows // TW
    kt = pmap.shape[1]
    loads[0].wait()
    sel = (iota((rows, pmap.shape[0]), 1) == tiles * pidx + div3(iota((rows, pmap.shape[0]), 0), 5)).astype(f32)
    mask8 = jnp.dot(sel, pmap[...].astype(f32), preferred_element_type=f32)

    def mask_of(first, width):
        spread = (div3(first + iota((kt, width), 1), 5) == iota((kt, width), 0)).astype(f32)
        return jnp.dot(mask8, spread, preferred_element_type=f32)

    kw = amp.shape[1]
    live_mask = mask_of(0, kw).astype(bf16)
    eye = (iota((kw, kw), 0) == iota((kw, kw), 1)).astype(bf16)
    loads[1].wait()
    amp[...] = amp[...] * live_mask
    ampt[...] = lax.dot_general(
        eye, amp[...], (((1,), (1,)), ((), ())), preferred_element_type=f32
    ).astype(bf16)
    loads[2].wait()

    half = kw // NY
    first = []
    for n, (c0, width, order) in enumerate(PARTS):
        d, r1, s1, r2, e, r3 = bufs[6 * n : 6 * n + 6]
        for yy in range(NY):
            block = jnp.dot(
                ampt[yy * half : (yy + 1) * half, :], lam[:, c0 : c0 + width],
                preferred_element_type=f32,
            ).astype(bf16)
            for xx in range(NX):
                piece = block[xx * TW : (xx + 1) * TW, :]
                if order == "x,y":
                    d[xx, yy] = piece
                else:
                    d[yy, xx] = piece
        if n == 0:
            pl.semaphore_wait(barrier, len(partners))
        if order == "x,y":
            first.append([send(d.at[xs(k)], r1.at[k - 1], at(y, xs(k), z)) for k in (2, 1, 3)])
        elif order == "y,x":
            first.append([send(d.at[1 - y], r1.at[0], at(1 - y, x, z))])
        else:
            first.append([
                send(d.at[lax.rem(y + dy, NY), xs(dx)], r1.at[k], at(lax.rem(y + dy, NY), xs(dx), z))
                for k, (dy, dx) in enumerate(offsets)
            ])

    loads[3].wait()
    wide = kw // NREP
    for r in range(NREP):
        part = lax.dot_general(
            lam[...], ints[r * wide : (r + 1) * wide, :], (((1,), (1,)), ((), ())),
            preferred_element_type=f32,
        )
        lpart[r] = (part * mask_of(r * wide, wide)).astype(bf16)
    lam_sends = [
        send(lpart.at[lax.rem(rep + k, NREP)], lrecv.at[k - 1], (pidx, lax.rem(rep + k, NREP)))
        for k in (1, 2, 3)
    ]
    ncol = lam.shape[1]
    for c0 in range(0, ncol, 384):
        lad[:, c0 : c0 + 384] = jnp.dot(
            amp[...], ints[:, c0 : c0 + 384], preferred_element_type=f32
        ).astype(bf16)
    lad_copy = pltpu.make_async_copy(lad, lad_o, lsem.at[4])
    lad_copy.start()

    spread_rows = iota((NZ * PAD, TW), 0)
    spread = (
        ((spread_rows >> 3) * OWN + (spread_rows & 7) == iota((NZ * PAD, TW), 1))
        & ((spread_rows & 7) < OWN)
    ).astype(bf16)

    def to_z(n, total):
        c0, width, order = PARTS[n]
        e, r3 = bufs[6 * n + 4 : 6 * n + 6]
        padded = jnp.dot(spread, total.astype(bf16), preferred_element_type=f32)
        e[...] = padded.reshape(NZ, PAD, width).astype(bf16)
        return [send(e.at[zs(k)], r3.at[k - 1], at(y, x, zs(k))) for k in zorder]

    second, third = {}, {}

    def stage_one(n):
        c0, width, order = PARTS[n]
        d, r1, s1, r2, e, r3 = bufs[6 * n : 6 * n + 6]
        for copy in first[n]:
            copy.wait()
        if order == "x,y":
            total = d[x].astype(f32) + r1[0].astype(f32) + r1[1].astype(f32) + r1[2].astype(f32)
            s1[...] = total.astype(bf16)
            second[n] = [send(s1.at[1 - y], r2.at[0], at(1 - y, x, z))]
        elif order == "y,x":
            s1[...] = (d[y].astype(f32) + r1[0].astype(f32)).astype(bf16)
            second[n] = [send(s1.at[xs(k)], r2.at[k - 1], at(y, xs(k), z)) for k in (2, 1, 3)]
        else:
            total = d[y, x].astype(f32)
            for k in range(len(offsets)):
                total += r1[k].astype(f32)
            third[n] = to_z(n, total)

    def stage_two(n):
        c0, width, order = PARTS[n]
        d, r1, s1, r2, e, r3 = bufs[6 * n : 6 * n + 6]
        if n not in second:
            return
        for copy in second[n]:
            copy.wait()
        if order == "x,y":
            total = s1[y].astype(f32) + r2[0].astype(f32)
        else:
            total = s1[x].astype(f32) + r2[0].astype(f32) + r2[1].astype(f32) + r2[2].astype(f32)
        third[n] = to_z(n, total)

    stage_one(0)
    stage_one(1)
    for n in range(2, len(PARTS)):
        stage_one(n)
        stage_two(n - 2)
    stage_two(len(PARTS) - 2)
    stage_two(len(PARTS) - 1)

    for copy in lam_sends:
        copy.wait()
    total = lpart[rep].astype(f32)
    for k in range(3):
        total += lrecv[k].astype(f32)
    ll_o[...] = total.astype(bf16)

    factor = 1.0 / (rows * NY * NX * NZ) ** 0.5
    for n, (c0, width, order) in enumerate(PARTS):
        e, r3 = bufs[6 * n + 4 : 6 * n + 6]
        for copy in third[n]:
            copy.wait()
        total = e[z].astype(f32)
        for k in range(NZ - 1):
            total += r3[k].astype(f32)
        den_o[:, c0 : c0 + width] = total * factor
    lad_copy.wait()


def body(amplitudes, lambda_amps, integrals, pair_map):
    rows, kw = amplitudes.shape
    ncol = lambda_amps.shape[1]
    wide = kw // NREP
    bf16 = jnp.bfloat16
    scratch = [
        pltpu.VMEM((rows, kw), bf16),
        pltpu.VMEM((rows, ncol), bf16),
        pltpu.VMEM((kw, ncol), bf16),
        pltpu.VMEM(pair_map.shape, jnp.int32),
        pltpu.VMEM((kw, rows), bf16),
        pltpu.VMEM((rows, ncol), bf16),
        pltpu.VMEM((NREP, rows, wide), bf16),
        pltpu.VMEM((NREP - 1, rows, wide), bf16),
    ]
    sends = 3
    parts = []
    for _, width, order in PARTS:
        if order == "x,y":
            shapes = [(NX, NY, TW), (NX - 1, NY, TW), (NY, TW), (1, TW)]
            sends += NX
        elif order == "y,x":
            shapes = [(NY, NX, TW), (1, NX, TW), (NX, TW), (NX - 1, TW)]
            sends += NX
        else:
            shapes = [(NY, NX, TW), (NX * NY - 1, TW), (16,), (16,)]
            sends += NX * NY - 1
        shapes += [(NZ, PAD), (NZ - 1, PAD)]
        sends += NZ - 1
        parts += [pltpu.VMEM(shape + (width,), bf16) for shape in shapes]
    scratch += [
        pltpu.SemaphoreType.DMA((5,)),
        pltpu.SemaphoreType.DMA((sends,)),
        pltpu.SemaphoreType.DMA((sends,)),
    ]
    anywhere = pl.BlockSpec(memory_space=pl.ANY)
    vmem = pl.BlockSpec(memory_space=pltpu.VMEM)
    ladder, summed, density = pl.pallas_call(
        kernel,
        out_shape=(
            jax.ShapeDtypeStruct((rows, ncol), bf16),
            jax.ShapeDtypeStruct((rows, wide), bf16),
            jax.ShapeDtypeStruct((PAD, ncol), jnp.float32),
        ),
        in_specs=[anywhere] * 4,
        out_specs=(anywhere, vmem, vmem),
        scratch_shapes=scratch + parts,
        compiler_params=pltpu.CompilerParams(
            collective_id=0, has_side_effects=True, vmem_limit_bytes=56 * 2**20
        ),
        cost_estimate=pl.CostEstimate(
            flops=6 * rows * kw * ncol, bytes_accessed=4 * 2**20, transcendentals=0
        ),
    )(amplitudes, lambda_amps, integrals, pair_map)
    return ladder, summed, density[:OWN]


def solution(mesh):
    in_specs = (P("pair", None), P("pair", "rep"), P(None, "rep"), P())
    out_specs = (P("pair", "rep"), P("pair", "rep"), P("pair", "rep"))
    return jax.shard_map(body, mesh=mesh, in_specs=in_specs, out_specs=out_specs, check_vma=False)
```

```python
import math

import jax
import jax.numpy as jnp
from jax import lax
from jax.experimental import pallas as pl
from jax.experimental.pallas import tpu as pltpu
from jax.sharding import PartitionSpec as P

TW = 96
NY, NX, NZ = 2, 4, 16
NREP = 4
OWN = 6
PAD = 8
MESH = pl.DeviceIdType.MESH
PARTS = (
    (0, 256, ("x", "y")),
    (256, 256, ("yx",)),
    (512, 256, ("p0", "x", "y")),
    (768, 384, ("p1", "yx")),
)
ORDER = ((0, 0), (2, 0), (3, 0), (1, 0), (0, 1), (2, 1), (3, 1), (2, 2))
CLOSE = (0, 1, 3, 2)


def axes_of(steps):
    sizes = {"x": (NX,), "y": (NY,), "yx": (NY, NX), "p0": (2,), "p1": (2,)}
    paired = "p0" in steps or "p1" in steps
    return [sizes[step] for step in steps], TW // 2 if paired else TW, NZ // 2 if paired else NZ


def div3(value, shift):
    return ((value >> shift) * 21846) >> 16


def kernel(amp_h, lam_h, int_h, pm_h, lad_o, ll_o, den_o, *scratch):
    (amp, lam, ints, pmap, ampt, ampp, lad, lpart, lrecv, lsem, ssem, rsem), bufs = scratch[:12], list(scratch[12:])
    pidx, rep = lax.axis_index("pair"), lax.axis_index("rep")
    z, x, y = lax.rem(pidx, NZ), lax.rem(pidx // NZ, NX), pidx // (NZ * NX)
    loads = [
        pltpu.make_async_copy(src, dst, lsem.at[k])
        for k, (src, dst) in enumerate(((pm_h, pmap), (amp_h, amp), (lam_h, lam), (int_h, ints)))
    ]
    for load in loads:
        load.start()

    def at(yy, xx, zz):
        return ((yy * NX + xx) * NZ + zz, rep)

    def xs(d):
        return lax.rem(x + d, NX)

    def zs(d):
        return lax.rem(z + d, NZ)

    offsets = [(dy, dx) for dx in (2, 1, 3, 0) for dy in (1, 0) if (dy, dx) != (0, 0)]
    zorder = (8, 7, 9, 6, 10, 5, 11, 4, 12, 3, 13, 2, 14, 1, 15)
    partners = [at(lax.rem(y + dy, NY), xs(dx), z) for dy, dx in offsets]
    partners += [at(y, x, zs(d)) for d in zorder]
    partners += [(pidx, lax.rem(rep + d, NREP)) for d in (1, 2, 3)]
    barrier = pltpu.get_barrier_semaphore()
    for device in partners:
        pl.semaphore_signal(barrier, inc=1, device_id=device, device_id_type=MESH)

    count = [0]

    def send(src, dst, device):
        k = count[0]
        count[0] += 1
        copy = pltpu.make_async_remote_copy(
            src_ref=src, dst_ref=dst, send_sem=ssem.at[k], recv_sem=rsem.at[k],
            device_id=device, device_id_type=MESH,
        )
        copy.start()
        return copy

    rows = amp.shape[0]
    f32, bf16 = jnp.float32, jnp.bfloat16

    def iota(shape, dim):
        return lax.broadcasted_iota(jnp.int32, shape, dim)

    tiles = rows // TW
    kt, ntiles = pmap.shape
    loads[0].wait()
    sel = (iota((rows, ntiles), 1) == tiles * pidx + div3(iota((rows, ntiles), 0), 5)).astype(f32)
    mask8 = lax.dot_general(
        sel, pmap[...].astype(f32), (((1,), (1,)), ((), ())), preferred_element_type=f32
    )

    def mask_of(first, width):
        spread = (div3(first + iota((kt, width), 1), 5) == iota((kt, width), 0)).astype(f32)
        return jnp.dot(mask8, spread, preferred_element_type=f32)

    kw = amp.shape[1]
    live_mask = mask_of(0, kw).astype(bf16)
    lanes, turned = iota((kw, kw), 1), iota((kw, 1), 0)
    eye = (turned == lanes).astype(bf16)
    odd = (turned >= kw // 2).astype(jnp.int32)
    inner = turned - odd * (kw // 2)
    sixth = div3(inner, 1)
    by_parity = (2 * OWN * sixth + OWN * odd + inner - OWN * sixth == lanes).astype(bf16)
    loads[1].wait()
    amp[...] = amp[...] * live_mask
    for order, dst in ((by_parity, ampp), (eye, ampt)):
        dst[...] = lax.dot_general(
            order, amp[...], (((1,), (1,)), ((), ())), preferred_element_type=f32
        ).astype(bf16)
    loads[2].wait()

    half = kw // 2
    zb = lax.rem(z, 2)
    mine = {"x": (x,), "y": (y,), "yx": (y, x), "p0": (zb,), "p1": (zb,)}
    peers = {
        "x": [((xs(k),), at(y, xs(k), z)) for k in (2, 1, 3)],
        "y": [((1 - y,), at(1 - y, x, z))],
        "yx": [
            ((lax.rem(y + dy, NY), xs(dx)), at(lax.rem(y + dy, NY), xs(dx), z)) for dy, dx in offsets
        ],
        "p0": [((1 - zb,), at(y, x, zs(NZ + 1 - 2 * zb)))],
        "p1": [((1 - zb,), at(y, x, zs(NZ - 1 + 2 * zb)))],
    }
    cur, recv, last, flying = [], [], [], []
    for c0, width, steps in PARTS:
        cur.append([bufs.pop(0) for _ in steps])
        recv.append([bufs.pop(0) for _ in steps])
        last.append((bufs.pop(0), bufs.pop(0)))
        flying.append(None)

    def launch(n, s):
        flying[n] = [
            send(cur[n][s].at[block], recv[n][s].at[k], device)
            for k, (block, device) in enumerate(peers[PARTS[n][2][s]])
        ]

    for n, (c0, width, steps) in enumerate(PARTS):
        axes, deep, members = axes_of(steps)
        paired = deep < TW
        for hi in range(2):
            block = jnp.dot(
                (ampp if paired else ampt)[hi * half : (hi + 1) * half, :], lam[:, c0 : c0 + width],
                preferred_element_type=f32,
            ).astype(bf16)
            for lo in range(half // deep):
                index = {"x": (lo % NX,), "p0": (hi,), "p1": (hi,)}
                index["y"] = (lo // NX if paired else hi,)
                index["yx"] = index["y"] + index["x"]
                where = sum((index[step] for step in steps), ())
                cur[n][0][where] = block[lo * deep : (lo + 1) * deep, :]
        if n == 0:
            pl.semaphore_wait(barrier, len(partners))
        launch(n, 0)

    loads[3].wait()
    wide = kw // NREP
    for r in range(NREP):
        part = lax.dot_general(
            lam[...], ints[r * wide : (r + 1) * wide, :], (((1,), (1,)), ((), ())),
            preferred_element_type=f32,
        )
        lpart[r] = (part * mask_of(r * wide, wide)).astype(bf16)
    lam_sends = [
        send(lpart.at[lax.rem(rep + k, NREP)], lrecv.at[k - 1], (pidx, lax.rem(rep + k, NREP)))
        for k in (1, 2, 3)
    ]
    ncol = lam.shape[1]
    for c0 in range(0, ncol, 384):
        lad[:, c0 : c0 + 384] = jnp.dot(
            amp[...], ints[:, c0 : c0 + 384], preferred_element_type=f32
        ).astype(bf16)
    lad_copy = pltpu.make_async_copy(lad, lad_o, lsem.at[4])
    lad_copy.start()

    def spread_of(members):
        spread_rows = iota((members * PAD, 1), 0)
        slot = spread_rows & (PAD - 1)
        source = jnp.where(slot < OWN, (spread_rows >> 3) * OWN + slot, -1)
        return (source == iota((members * PAD, members * OWN), 1)).astype(bf16)

    def finish_step(n, s):
        c0, width, steps = PARTS[n]
        axes, deep, members = axes_of(steps)
        for copy in flying[n]:
            copy.wait()
        total = cur[n][s][mine[steps[s]]].astype(f32)
        for k in range(len(flying[n])):
            total += recv[n][s][k].astype(f32)
        if s + 1 < len(steps):
            cur[n][s + 1][...] = total.astype(bf16)
            launch(n, s + 1)
            return
        out, into = last[n]
        padded = jnp.dot(spread_of(members), total.astype(bf16), preferred_element_type=f32)
        out[...] = padded.reshape(members, PAD, width).astype(bf16)
        step = NZ // members
        place = z // step
        flying[n] = [
            send(out.at[lax.rem(place + k, members)], into.at[k - 1], at(y, x, zs(k * step)))
            for k in sorted(range(1, members), key=lambda k: -min(k, members - k))
        ]

    for n, s in ORDER:
        finish_step(n, s)

    for copy in lam_sends:
        copy.wait()
    total = lpart[rep].astype(f32)
    for k in range(3):
        total += lrecv[k].astype(f32)
    ll_o[...] = total.astype(bf16)

    factor = 1.0 / (rows * NY * NX * NZ) ** 0.5
    for n in CLOSE:
        c0, width, steps = PARTS[n]
        out, into = last[n]
        members = out.shape[0]
        for copy in flying[n]:
            copy.wait()
        total = out[z // (NZ // members)].astype(f32)
        for k in range(members - 1):
            total += into[k].astype(f32)
        den_o[:, c0 : c0 + width] = total * factor
    lad_copy.wait()


def finish(lad_i, ll_i, den_i, lad_o, ll_o, den_o):
    lad_o[...] = lad_i[...]
    ll_o[...] = ll_i[...]
    den_o[...] = den_i[:OWN, :]


def body(amplitudes, lambda_amps, integrals, pair_map):
    rows, kw = amplitudes.shape
    ncol = lambda_amps.shape[1]
    wide = kw // NREP
    bf16 = jnp.bfloat16
    scratch = [
        pltpu.VMEM((rows, kw), bf16),
        pltpu.VMEM((rows, ncol), bf16),
        pltpu.VMEM((kw, ncol), bf16),
        pltpu.VMEM(pair_map.shape[::-1], jnp.int32),
        pltpu.VMEM((kw, rows), bf16),
        pltpu.VMEM((kw, rows), bf16),
        pltpu.VMEM((rows, ncol), bf16),
        pltpu.VMEM((NREP, rows, wide), bf16),
        pltpu.VMEM((NREP - 1, rows, wide), bf16),
    ]
    sends = 3
    parts = []
    for _, width, steps in PARTS:
        axes, deep, members = axes_of(steps)
        dims = [sum(axes[s:], ()) + (deep,) for s in range(len(steps))]
        shapes = dims + [
            (math.prod(axes[s]) - 1,) + sum(axes[s + 1 :], ()) + (deep,) for s in range(len(steps))
        ]
        sends += sum(math.prod(axis) - 1 for axis in axes) + members - 1
        shapes += [(members, PAD), (members - 1, PAD)]
        parts += [pltpu.VMEM(shape + (width,), bf16) for shape in shapes]
    scratch += [
        pltpu.SemaphoreType.DMA((5,)),
        pltpu.SemaphoreType.DMA((sends,)),
        pltpu.SemaphoreType.DMA((sends,)),
    ]
    anywhere = pl.BlockSpec(memory_space=pl.ANY)
    vmem = pl.BlockSpec(memory_space=pltpu.VMEM)
    ladder, summed, density = pl.pallas_call(
        kernel,
        out_shape=(
            jax.ShapeDtypeStruct((rows, ncol), bf16),
            jax.ShapeDtypeStruct((rows, wide), bf16),
            jax.ShapeDtypeStruct((PAD, ncol), jnp.float32),
        ),
        in_specs=[anywhere] * 4,
        out_specs=(anywhere, vmem, vmem),
        scratch_shapes=scratch + parts,
        compiler_params=pltpu.CompilerParams(
            collective_id=0, has_side_effects=True, vmem_limit_bytes=56 * 2**20
        ),
        cost_estimate=pl.CostEstimate(
            flops=6 * rows * kw * ncol, bytes_accessed=4 * 2**20, transcendentals=0
        ),
    )(amplitudes, lambda_amps, integrals, pair_map.T)
    return pl.pallas_call(
        finish,
        out_shape=(
            jax.ShapeDtypeStruct((rows, ncol), bf16),
            jax.ShapeDtypeStruct((rows, wide), bf16),
            jax.ShapeDtypeStruct((OWN, ncol), jnp.float32),
        ),
        in_specs=[vmem] * 3,
        out_specs=(vmem,) * 3,
    )(ladder, summed, density)


def solution(mesh):
    in_specs = (P("pair", None), P("pair", "rep"), P(None, "rep"), P())
    out_specs = (P("pair", "rep"), P("pair", "rep"), P("pair", "rep"))
    return jax.shard_map(body, mesh=mesh, in_specs=in_specs, out_specs=out_specs, check_vma=False)
```

```python
import math

import jax
import jax.numpy as jnp
from jax import lax
from jax.experimental import pallas as pl
from jax.experimental.pallas import tpu as pltpu
from jax.sharding import PartitionSpec as P

TW = 96
NY, NX, NZ = 2, 4, 16
NREP = 4
OWN = 6
PAD = 8
MESH = pl.DeviceIdType.MESH
PARTS = (
    (0, 256, ("p0", "yx")),
    (256, 256, ("yx",)),
    (512, 128, ("yx",)),
    (640, 128, ("p1", "yx")),
    (768, 128, ("p1", "yx")),
    (896, 128, ("p0", "yx")),
    (1024, 128, ("p1", "yx")),
)
ORDER = ((3, 0), (0, 0), (4, 0), (5, 0), (1, 0), (6, 0), (2, 0), (3, 1), (0, 1), (4, 1), (5, 1), (6, 1))
CLOSE = (1, 2, 3, 0, 4, 5, 6)
START = (1, 2, 0, 3, 4, 5, 6)
LAMBDA_AT = (2, 10)


def axes_of(steps):
    sizes = {"x": (NX,), "y": (NY,), "yx": (NY, NX), "p0": (2,), "p1": (2,)}
    paired = "p0" in steps or "p1" in steps
    return [sizes[step] for step in steps], TW // 2 if paired else TW, NZ // 2 if paired else NZ


def div3(value, shift):
    return ((value >> shift) * 21846) >> 16


def kernel(amp_h, lam_h, int_h, pm_h, lad_o, ll_o, den_o, *scratch):
    (amp, lam, ints, pmap, ampt, ampp, lad, lpart, lrecv, lsum, lfar, lsem, ssem, rsem, known), bufs = scratch[:15], list(scratch[15:])
    pidx, rep = lax.axis_index("pair"), lax.axis_index("rep")
    z, x, y = lax.rem(pidx, NZ), lax.rem(pidx // NZ, NX), pidx // (NZ * NX)
    loads = [
        pltpu.make_async_copy(src, dst, lsem.at[k])
        for k, (src, dst) in enumerate(((pm_h, pmap), (amp_h, amp), (lam_h, lam), (int_h, ints)))
    ]
    for load in loads[:3]:
        load.start()

    def at(yy, xx, zz):
        return ((yy * NX + xx) * NZ + zz, rep)

    def xs(d):
        return lax.rem(x + d, NX)

    def zs(d):
        return lax.rem(z + d, NZ)

    offsets = [(dy, dx) for dx in (2, 1, 3, 0) for dy in (1, 0) if (dy, dx) != (0, 0)]
    partners = [at(lax.rem(y + dy, NY), xs(dx), z) for dy, dx in offsets]
    partners += [at(y, x, zs(d)) for d in (1, NZ - 1)]
    core, ylo = lax.rem(rep, 2), rep // 2
    partners += [(pidx, 2 * ylo + 1 - core), (pidx, 2 * (1 - ylo) + core)]
    barrier = pltpu.get_barrier_semaphore()
    for device in partners:
        pl.semaphore_signal(barrier, inc=1, device_id=device, device_id_type=MESH)

    def greet(level):
        for d in (2**level, NZ - 2**level):
            pl.semaphore_signal(
                known.at[level], inc=1, device_id=at(y, x, zs(d)), device_id_type=MESH
            )

    count = [0]

    def send(src, dst, device):
        k = count[0]
        count[0] += 1
        copy = pltpu.make_async_remote_copy(
            src_ref=src, dst_ref=dst, send_sem=ssem.at[k], recv_sem=rsem.at[k],
            device_id=device, device_id_type=MESH,
        )
        copy.start()
        return copy

    rows = amp.shape[0]
    f32, bf16 = jnp.float32, jnp.bfloat16

    def iota(shape, dim):
        return lax.broadcasted_iota(jnp.int32, shape, dim)

    tiles = rows // TW
    kt, ntiles = pmap.shape
    loads[0].wait()
    sel = (iota((rows, ntiles), 1) == tiles * pidx + div3(iota((rows, ntiles), 0), 5)).astype(bf16)
    mask8 = lax.dot_general(
        sel, pmap[...].astype(bf16), (((1,), (1,)), ((), ())), preferred_element_type=f32
    ).astype(bf16)

    def mask_of(first, width):
        spread = (div3(first + iota((kt, width), 1), 5) == iota((kt, width), 0)).astype(bf16)
        return jnp.dot(mask8, spread, preferred_element_type=f32)

    kw = amp.shape[1]
    live_mask = mask_of(0, kw).astype(bf16)
    blk = 256
    eye = (iota((blk, 1), 0) == iota((blk, blk), 1)).astype(bf16)
    loads[1].wait()
    amp[...] = amp[...] * live_mask

    def turn(order, columns):
        return lax.dot_general(
            order, amp[:, columns], (((1,), (1,)), ((), ())), preferred_element_type=f32
        ).astype(bf16)

    for c0 in range(0, kw, blk):
        ampt[c0 : c0 + blk, :] = turn(eye, slice(c0, c0 + blk))
    loads[2].wait()
    loads[3].start()

    half = kw // 2
    zb = lax.rem(z, 2)
    mine = {"x": (x,), "y": (y,), "yx": (y, x), "p0": (zb,), "p1": (zb,)}
    peers = {
        "x": [((xs(k),), at(y, xs(k), z)) for k in (2, 1, 3)],
        "y": [((1 - y,), at(1 - y, x, z))],
        "yx": [
            ((lax.rem(y + dy, NY), xs(dx)), at(lax.rem(y + dy, NY), xs(dx), z)) for dy, dx in offsets
        ],
        "p0": [((1 - zb,), at(y, x, zs(NZ + 1 - 2 * zb)))],
        "p1": [((1 - zb,), at(y, x, zs(NZ - 1 + 2 * zb)))],
    }
    cur, recv, last, flying = [], [], [], []
    for c0, width, steps in PARTS:
        cur.append([bufs.pop(0) for _ in steps])
        recv.append([bufs.pop(0) for _ in steps])
        last.append((bufs.pop(0), bufs.pop(0)))
        flying.append(None)

    def launch(n, s):
        flying[n] = [
            send(cur[n][s].at[block], recv[n][s].at[k], device)
            for k, (block, device) in enumerate(peers[PARTS[n][2][s]])
        ]

    def split_rows():
        quarter = kw // 4
        for hi in range(2):
            for lo in range(2):
                inner = iota((quarter, 1), 0)
                sixth = div3(inner, 1)
                source = 2 * OWN * sixth + OWN * hi + inner - OWN * sixth
                order = (source == iota((quarter, half), 1)).astype(bf16)
                r0 = hi * half + lo * quarter
                ampp[r0 : r0 + quarter, :] = turn(order, slice(lo * half, lo * half + half))

    split = False
    for n in START:
        c0, width, steps = PARTS[n]
        axes, deep, members = axes_of(steps)
        paired = deep < TW
        if paired and not split:
            split_rows()
            split = True
        for hi in range(2):
            block = jnp.dot(
                (ampp if paired else ampt)[hi * half : (hi + 1) * half, :], lam[:, c0 : c0 + width],
                preferred_element_type=f32,
            ).astype(bf16)
            for lo in range(half // deep):
                index = {"x": (lo % NX,), "p0": (hi,), "p1": (hi,)}
                index["y"] = (lo // NX if paired else hi,)
                index["yx"] = index["y"] + index["x"]
                where = sum((index[step] for step in steps), ())
                cur[n][0][where] = block[lo * deep : (lo + 1) * deep, :]
        if n == START[0]:
            pl.semaphore_wait(barrier, len(partners))
            greet(0)
        launch(n, 0)

    pl.semaphore_wait(known.at[0], 2)
    greet(1)
    loads[3].wait()
    wide = kw // NREP
    for r in range(NREP):
        part = lax.dot_general(
            lam[...], ints[r * wide : (r + 1) * wide, :], (((1,), (1,)), ((), ())),
            preferred_element_type=f32,
        )
        lpart[r % 2, r // 2] = (part * mask_of(r * wide, wide)).astype(bf16)
    over_core = send(lpart.at[1 - core], lrecv, (pidx, 2 * ylo + 1 - core))
    pl.semaphore_wait(known.at[1], 2)
    greet(2)
    ncol = lam.shape[1]
    for c0 in range(0, ncol, 384):
        lad[:, c0 : c0 + 384] = jnp.dot(
            amp[...], ints[:, c0 : c0 + 384], preferred_element_type=f32
        ).astype(bf16)
    lad_copy = pltpu.make_async_copy(lad, lad_o, lsem.at[4])
    lad_copy.start()

    pl.semaphore_wait(known.at[2], 2)

    def spread_of(members):
        spread_rows = iota((members * PAD, 1), 0)
        slot = spread_rows & (PAD - 1)
        source = jnp.where(slot < OWN, (spread_rows >> 3) * OWN + slot, -1)
        return (source == iota((members * PAD, members * OWN), 1)).astype(bf16)

    def finish_step(n, s):
        c0, width, steps = PARTS[n]
        axes, deep, members = axes_of(steps)
        for copy in flying[n]:
            copy.wait()
        total = cur[n][s][mine[steps[s]]].astype(f32)
        for k in range(len(flying[n])):
            total += recv[n][s][k].astype(f32)
        if s + 1 < len(steps):
            cur[n][s + 1][...] = total.astype(bf16)
            launch(n, s + 1)
            return
        out, into = last[n]
        padded = jnp.dot(spread_of(members), total.astype(bf16), preferred_element_type=f32)
        out[...] = padded.reshape(members, PAD, width).astype(bf16)
        step = NZ // members
        place = z // step
        flying[n] = [
            send(out.at[lax.rem(place + k, members)], into.at[k - 1], at(y, x, zs(k * step)))
            for k in sorted(range(1, members), key=lambda k: -min(k, members - k))
        ]

    for k, (n, s) in enumerate(ORDER):
        if k == LAMBDA_AT[0]:
            over_core.wait()
            lsum[...] = (lpart[core].astype(f32) + lrecv[...].astype(f32)).astype(bf16)
        if k == LAMBDA_AT[1]:
            over_y = send(lsum.at[1 - ylo], lfar, (pidx, 2 * (1 - ylo) + core))
        finish_step(n, s)

    over_y.wait()
    ll_o[...] = (lsum[ylo].astype(f32) + lfar[...].astype(f32)).astype(bf16)

    factor = 1.0 / (rows * NY * NX * NZ) ** 0.5
    for n in CLOSE:
        c0, width, steps = PARTS[n]
        out, into = last[n]
        members = out.shape[0]
        for copy in flying[n]:
            copy.wait()
        total = out[z // (NZ // members)].astype(f32)
        for k in range(members - 1):
            total += into[k].astype(f32)
        den_o[:, c0 : c0 + width] = total * factor
    lad_copy.wait()


def finish(lad_i, ll_i, den_i, lad_o, ll_o, den_o):
    lad_o[...] = lad_i[...]
    ll_o[...] = ll_i[...]
    den_o[...] = den_i[:OWN, :]


def body(amplitudes, lambda_amps, integrals, pair_map):
    rows, kw = amplitudes.shape
    ncol = lambda_amps.shape[1]
    wide = kw // NREP
    bf16 = jnp.bfloat16
    scratch = [
        pltpu.VMEM((rows, kw), bf16),
        pltpu.VMEM((rows, ncol), bf16),
        pltpu.VMEM((kw, ncol), bf16),
        pltpu.VMEM(pair_map.shape[::-1], jnp.int32),
        pltpu.VMEM((kw, rows), bf16),
        pltpu.VMEM((kw, rows), bf16),
        pltpu.VMEM((rows, ncol), bf16),
        pltpu.VMEM((2, NREP // 2, rows, wide), bf16),
        pltpu.VMEM((NREP // 2, rows, wide), bf16),
        pltpu.VMEM((NREP // 2, rows, wide), bf16),
        pltpu.VMEM((rows, wide), bf16),
    ]
    sends = 2
    parts = []
    for _, width, steps in PARTS:
        axes, deep, members = axes_of(steps)
        dims = [sum(axes[s:], ()) + (deep,) for s in range(len(steps))]
        shapes = dims + [
            (math.prod(axes[s]) - 1,) + sum(axes[s + 1 :], ()) + (deep,) for s in range(len(steps))
        ]
        sends += sum(math.prod(axis) - 1 for axis in axes) + members - 1
        shapes += [(members, PAD), (members - 1, PAD)]
        parts += [pltpu.VMEM(shape + (width,), bf16) for shape in shapes]
    scratch += [
        pltpu.SemaphoreType.DMA((5,)),
        pltpu.SemaphoreType.DMA((sends,)),
        pltpu.SemaphoreType.DMA((sends,)),
        pltpu.SemaphoreType.REGULAR((3,)),
    ]
    anywhere = pl.BlockSpec(memory_space=pl.ANY)
    vmem = pl.BlockSpec(memory_space=pltpu.VMEM)
    ladder, summed, density = pl.pallas_call(
        kernel,
        out_shape=(
            jax.ShapeDtypeStruct((rows, ncol), bf16),
            jax.ShapeDtypeStruct((rows, wide), bf16),
            jax.ShapeDtypeStruct((PAD, ncol), jnp.float32),
        ),
        in_specs=[anywhere] * 4,
        out_specs=(anywhere, vmem, vmem),
        scratch_shapes=scratch + parts,
        compiler_params=pltpu.CompilerParams(
            collective_id=0, has_side_effects=True, vmem_limit_bytes=56 * 2**20
        ),
        cost_estimate=pl.CostEstimate(
            flops=6 * rows * kw * ncol, bytes_accessed=4 * 2**20, transcendentals=0
        ),
    )(amplitudes, lambda_amps, integrals, pair_map.T)
    return pl.pallas_call(
        finish,
        out_shape=(
            jax.ShapeDtypeStruct((rows, ncol), bf16),
            jax.ShapeDtypeStruct((rows, wide), bf16),
            jax.ShapeDtypeStruct((OWN, ncol), jnp.float32),
        ),
        in_specs=[vmem] * 3,
        out_specs=(vmem,) * 3,
    )(ladder, summed, density)


def solution(mesh):
    in_specs = (P("pair", None), P("pair", "rep"), P(None, "rep"), P())
    out_specs = (P("pair", "rep"), P("pair", "rep"), P("pair", "rep"))
    return jax.shard_map(body, mesh=mesh, in_specs=in_specs, out_specs=out_specs, check_vma=False)
```

```python
import math

import jax
import jax.numpy as jnp
from jax import lax
from jax.experimental import pallas as pl
from jax.experimental.pallas import tpu as pltpu
from jax.sharding import PartitionSpec as P

TW = 96
NY, NX, NZ = 2, 4, 16
NREP = 4
OWN = 6
PAD = 8
MESH = pl.DeviceIdType.MESH
PARTS = (
    (0, 256, ("p0", "yx")),
    (256, 256, ("yx",)),
    (512, 128, ("yx",)),
    (640, 128, ("p1", "yx")),
    (768, 128, ("p1", "yx")),
    (896, 128, ("p0", "yx")),
    (1024, 128, ("p1", "yx")),
)
ORDER = ((3, 0), (0, 0), (4, 0), (5, 0), (1, 0), (6, 0), (2, 0), (3, 1), (0, 1), (4, 1), (5, 1), (6, 1))
CLOSE = (1, 2, 3, 0, 4, 5, 6)
START = (1, 2, 0, 3, 4, 5, 6)
LAMBDA_AT = (2, 10)


def axes_of(steps):
    sizes = {"x": (NX,), "y": (NY,), "yx": (NY, NX), "p0": (2,), "p1": (2,)}
    paired = "p0" in steps or "p1" in steps
    return [sizes[step] for step in steps], TW // 2 if paired else TW, NZ // 2 if paired else NZ


def div3(value, shift):
    return ((value >> shift) * 21846) >> 16


def kernel(amp_h, lam_h, int_h, pm_h, lad_o, ll_o, den_o, *scratch):
    (amp, lam, ints, pmap, ampt, ampp, lad, lpart, lrecv, lsum, lfar, lsem, ssem, rsem, known), bufs = scratch[:15], list(scratch[15:])
    pidx, rep = lax.axis_index("pair"), lax.axis_index("rep")
    z, x, y = lax.rem(pidx, NZ), lax.rem(pidx // NZ, NX), pidx // (NZ * NX)
    loads = [
        pltpu.make_async_copy(src, dst, lsem.at[k])
        for k, (src, dst) in enumerate(((pm_h, pmap), (amp_h, amp), (lam_h, lam), (int_h, ints)))
    ]
    for load in loads[:3]:
        load.start()

    def at(yy, xx, zz):
        return ((yy * NX + xx) * NZ + zz, rep)

    def xs(d):
        return lax.rem(x + d, NX)

    def zs(d):
        return lax.rem(z + d, NZ)

    offsets = [(dy, dx) for dx in (2, 1, 3, 0) for dy in (1, 0) if (dy, dx) != (0, 0)]
    partners = [at(lax.rem(y + dy, NY), xs(dx), z) for dy, dx in offsets]
    partners += [at(y, x, zs(d)) for d in (1, NZ - 1)]
    core, ylo = lax.rem(rep, 2), rep // 2
    partners += [(pidx, 2 * ylo + 1 - core), (pidx, 2 * (1 - ylo) + core)]
    barrier = pltpu.get_barrier_semaphore()
    for device in partners:
        pl.semaphore_signal(barrier, inc=1, device_id=device, device_id_type=MESH)

    def greet(level):
        for d in (2**level, NZ - 2**level):
            pl.semaphore_signal(
                known.at[level], inc=1, device_id=at(y, x, zs(d)), device_id_type=MESH
            )

    count = [0]

    def send(blocks, into):
        k = count[0]
        count[0] += 1

        def copy_of(src, dst, device):
            return pltpu.make_async_remote_copy(
                src_ref=src, dst_ref=dst, send_sem=ssem.at[k], recv_sem=rsem.at[k],
                device_id=device, device_id_type=MESH,
            )

        for src, dst, device in blocks:
            copy_of(src, dst, device).start()
        return copy_of(into, into, blocks[0][2])

    rows = amp.shape[0]
    f32, bf16 = jnp.float32, jnp.bfloat16

    def iota(shape, dim):
        return lax.broadcasted_iota(jnp.int32, shape, dim)

    tiles = rows // TW
    kt, ntiles = pmap.shape
    loads[0].wait()
    sel = (iota((rows, ntiles), 1) == tiles * pidx + div3(iota((rows, ntiles), 0), 5)).astype(bf16)
    mask8 = lax.dot_general(
        sel, pmap[...].astype(bf16), (((1,), (1,)), ((), ())), preferred_element_type=f32
    ).astype(bf16)

    def mask_of(first, width):
        spread = (div3(first + iota((kt, width), 1), 5) == iota((kt, width), 0)).astype(bf16)
        return jnp.dot(mask8, spread, preferred_element_type=f32)

    kw = amp.shape[1]
    live_mask = mask_of(0, kw).astype(bf16)
    blk = 256
    eye = (iota((blk, 1), 0) == iota((blk, blk), 1)).astype(bf16)
    loads[1].wait()
    amp[...] = amp[...] * live_mask

    def turn(order, columns):
        return lax.dot_general(
            order, amp[:, columns], (((1,), (1,)), ((), ())), preferred_element_type=f32
        ).astype(bf16)

    for c0 in range(0, kw, blk):
        ampt[c0 : c0 + blk, :] = turn(eye, slice(c0, c0 + blk))
    loads[2].wait()
    loads[3].start()

    half = kw // 2
    zb = lax.rem(z, 2)
    mine = {"x": (x,), "y": (y,), "yx": (y, x), "p0": (zb,), "p1": (zb,)}
    peers = {
        "x": [((xs(k),), at(y, xs(k), z)) for k in (2, 1, 3)],
        "y": [((1 - y,), at(1 - y, x, z))],
        "yx": [
            ((lax.rem(y + dy, NY), xs(dx)), at(lax.rem(y + dy, NY), xs(dx), z)) for dy, dx in offsets
        ],
        "p0": [((1 - zb,), at(y, x, zs(NZ + 1 - 2 * zb)))],
        "p1": [((1 - zb,), at(y, x, zs(NZ - 1 + 2 * zb)))],
    }
    cur, recv, last, flying, flown = [], [], [], [], []
    for c0, width, steps in PARTS:
        cur.append([bufs.pop(0) for _ in steps])
        recv.append([bufs.pop(0) for _ in steps])
        last.append((bufs.pop(0), bufs.pop(0)))
        flying.append(None)

    def launch(n, s):
        into = recv[n][s]
        flying[n] = send(
            [
                (cur[n][s].at[block], into.at[k], device)
                for k, (block, device) in enumerate(peers[PARTS[n][2][s]])
            ],
            into,
        )

    def split_rows():
        quarter = kw // 4
        for hi in range(2):
            for lo in range(2):
                inner = iota((quarter, 1), 0)
                sixth = div3(inner, 1)
                source = 2 * OWN * sixth + OWN * hi + inner - OWN * sixth
                order = (source == iota((quarter, half), 1)).astype(bf16)
                r0 = hi * half + lo * quarter
                ampp[r0 : r0 + quarter, :] = turn(order, slice(lo * half, lo * half + half))

    split = False
    for n in START:
        c0, width, steps = PARTS[n]
        axes, deep, members = axes_of(steps)
        paired = deep < TW
        if paired and not split:
            split_rows()
            split = True
        for hi in range(2):
            block = jnp.dot(
                (ampp if paired else ampt)[hi * half : (hi + 1) * half, :], lam[:, c0 : c0 + width],
                preferred_element_type=f32,
            ).astype(bf16)
            for lo in range(half // deep):
                index = {"x": (lo % NX,), "p0": (hi,), "p1": (hi,)}
                index["y"] = (lo // NX if paired else hi,)
                index["yx"] = index["y"] + index["x"]
                where = sum((index[step] for step in steps), ())
                cur[n][0][where] = block[lo * deep : (lo + 1) * deep, :]
        if n == START[0]:
            pl.semaphore_wait(barrier, len(partners))
            greet(0)
        launch(n, 0)

    pl.semaphore_wait(known.at[0], 2)
    greet(1)
    loads[3].wait()
    wide = kw // NREP
    for r in range(NREP):
        part = lax.dot_general(
            lam[...], ints[r * wide : (r + 1) * wide, :], (((1,), (1,)), ((), ())),
            preferred_element_type=f32,
        )
        lpart[r % 2, r // 2] = (part * mask_of(r * wide, wide)).astype(bf16)
    over_core = send([(lpart.at[1 - core], lrecv, (pidx, 2 * ylo + 1 - core))], lrecv)
    pl.semaphore_wait(known.at[1], 2)
    greet(2)
    ncol = lam.shape[1]
    for c0 in range(0, ncol, 384):
        lad[:, c0 : c0 + 384] = jnp.dot(
            amp[...], ints[:, c0 : c0 + 384], preferred_element_type=f32
        ).astype(bf16)
    lad_copy = pltpu.make_async_copy(lad, lad_o, lsem.at[4])
    lad_copy.start()

    pl.semaphore_wait(known.at[2], 2)

    def spread_of(members):
        spread_rows = iota((members * PAD, 1), 0)
        slot = spread_rows & (PAD - 1)
        source = jnp.where(slot < OWN, (spread_rows >> 3) * OWN + slot, -1)
        return (source == iota((members * PAD, members * OWN), 1)).astype(bf16)

    def finish_step(n, s):
        c0, width, steps = PARTS[n]
        axes, deep, members = axes_of(steps)
        flying[n].wait_recv()
        flown.append(flying[n])
        total = cur[n][s][mine[steps[s]]].astype(f32)
        for k in range(recv[n][s].shape[0]):
            total += recv[n][s][k].astype(f32)
        if s + 1 < len(steps):
            cur[n][s + 1][...] = total.astype(bf16)
            launch(n, s + 1)
            return
        out, into = last[n]
        padded = jnp.dot(spread_of(members), total.astype(bf16), preferred_element_type=f32)
        out[...] = padded.reshape(members, PAD, width)[:, :OWN, :].astype(bf16)
        step = NZ // members
        place = z // step
        flying[n] = send(
            [
                (out.at[lax.rem(place + k, members)], into.at[k - 1], at(y, x, zs(k * step)))
                for k in sorted(range(1, members), key=lambda k: -min(k, members - k))
            ],
            into,
        )

    for k, (n, s) in enumerate(ORDER):
        if k == LAMBDA_AT[0]:
            over_core.wait()
            lsum[...] = (lpart[core].astype(f32) + lrecv[...].astype(f32)).astype(bf16)
        if k == LAMBDA_AT[1]:
            over_y = send([(lsum.at[1 - ylo], lfar, (pidx, 2 * (1 - ylo) + core))], lfar)
        finish_step(n, s)

    over_y.wait()
    for copies in flown:
        copies.wait_send()
    ll_o[...] = (lsum[ylo].astype(f32) + lfar[...].astype(f32)).astype(bf16)

    factor = 1.0 / (rows * NY * NX * NZ) ** 0.5
    for n in CLOSE:
        c0, width, steps = PARTS[n]
        out, into = last[n]
        members = out.shape[0]
        flying[n].wait()
        total = out[z // (NZ // members)].astype(f32)
        for k in range(members - 1):
            total += into[k].astype(f32)
        den_o[:, c0 : c0 + width] = total * factor
    lad_copy.wait()


def finish(lad_i, ll_i, den_i, lad_o, ll_o, den_o):
    lad_o[...] = lad_i[...]
    ll_o[...] = ll_i[...]
    den_o[...] = den_i[...]


def body(amplitudes, lambda_amps, integrals, pair_map):
    rows, kw = amplitudes.shape
    ncol = lambda_amps.shape[1]
    wide = kw // NREP
    bf16 = jnp.bfloat16
    scratch = [
        pltpu.VMEM((rows, kw), bf16),
        pltpu.VMEM((rows, ncol), bf16),
        pltpu.VMEM((kw, ncol), bf16),
        pltpu.VMEM(pair_map.shape[::-1], jnp.int32),
        pltpu.VMEM((kw, rows), bf16),
        pltpu.VMEM((kw, rows), bf16),
        pltpu.VMEM((rows, ncol), bf16),
        pltpu.VMEM((2, NREP // 2, rows, wide), bf16),
        pltpu.VMEM((NREP // 2, rows, wide), bf16),
        pltpu.VMEM((NREP // 2, rows, wide), bf16),
        pltpu.VMEM((rows, wide), bf16),
    ]
    sends = 2
    parts = []
    for _, width, steps in PARTS:
        axes, deep, members = axes_of(steps)
        dims = [sum(axes[s:], ()) + (deep,) for s in range(len(steps))]
        shapes = dims + [
            (math.prod(axes[s]) - 1,) + sum(axes[s + 1 :], ()) + (deep,) for s in range(len(steps))
        ]
        sends += len(steps) + 1
        shapes += [(members, OWN), (members - 1, OWN)]
        parts += [pltpu.VMEM(shape + (width,), bf16) for shape in shapes]
    scratch += [
        pltpu.SemaphoreType.DMA((5,)),
        pltpu.SemaphoreType.DMA((sends,)),
        pltpu.SemaphoreType.DMA((sends,)),
        pltpu.SemaphoreType.REGULAR((3,)),
    ]
    anywhere = pl.BlockSpec(memory_space=pl.ANY)
    vmem = pl.BlockSpec(memory_space=pltpu.VMEM)
    ladder, summed, density = pl.pallas_call(
        kernel,
        out_shape=(
            jax.ShapeDtypeStruct((rows, ncol), bf16),
            jax.ShapeDtypeStruct((rows, wide), bf16),
            jax.ShapeDtypeStruct((OWN, ncol), jnp.float32),
        ),
        in_specs=[anywhere] * 4,
        out_specs=(anywhere, vmem, vmem),
        scratch_shapes=scratch + parts,
        compiler_params=pltpu.CompilerParams(
            collective_id=0, has_side_effects=True, vmem_limit_bytes=56 * 2**20
        ),
        cost_estimate=pl.CostEstimate(
            flops=6 * rows * kw * ncol, bytes_accessed=4 * 2**20, transcendentals=0
        ),
    )(amplitudes, lambda_amps, integrals, pair_map.T)
    return pl.pallas_call(
        finish,
        out_shape=(
            jax.ShapeDtypeStruct((rows, ncol), bf16),
            jax.ShapeDtypeStruct((rows, wide), bf16),
            jax.ShapeDtypeStruct((OWN, ncol), jnp.float32),
        ),
        in_specs=[vmem] * 3,
        out_specs=(vmem,) * 3,
    )(ladder, summed, density)


def solution(mesh):
    in_specs = (P("pair", None), P("pair", "rep"), P(None, "rep"), P())
    out_specs = (P("pair", "rep"), P("pair", "rep"), P("pair", "rep"))
    return jax.shard_map(body, mesh=mesh, in_specs=in_specs, out_specs=out_specs, check_vma=False)
```

```python
import math

import jax
import jax.numpy as jnp
from jax import lax
from jax.experimental import pallas as pl
from jax.experimental.pallas import tpu as pltpu
from jax.sharding import PartitionSpec as P

TW = 96
NY, NX, NZ = 2, 4, 16
NREP = 4
OWN = 6
PAD = 8
MESH = pl.DeviceIdType.MESH
PARTS = (
    (0, 256, ("p0", "yx")),
    (256, 384, ("yx",)),
    (640, 256, ("p1", "yx")),
    (896, 128, ("p0", "yx")),
    (1024, 128, ("p1", "yx")),
)
ORDER = ((0, 0), (2, 0), (3, 0), (4, 0), (1, 0), (0, 1), (2, 1), (3, 1), (4, 1))
CLOSE = (1, 0, 2, 3, 4)
START = (1, 0, 2, 3, 4)
LAMBDA_AT = (2, 7)


def axes_of(steps):
    sizes = {"x": (NX,), "y": (NY,), "yx": (NY, NX), "p0": (2,), "p1": (2,)}
    paired = "p0" in steps or "p1" in steps
    return [sizes[step] for step in steps], TW // 2 if paired else TW, NZ // 2 if paired else NZ


def div3(value, shift):
    return ((value >> shift) * 21846) >> 16


def kernel(amp_h, lam_h, int_h, pm_h, lad_o, ll_o, den_o, *scratch):
    (amp, lam, ints, pmap, ampt, ampp, lad, lpart, lrecv, lsum, lfar, lsem, ssem, rsem, known), bufs = scratch[:15], list(scratch[15:])
    pidx, rep = lax.axis_index("pair"), lax.axis_index("rep")
    z, x, y = lax.rem(pidx, NZ), lax.rem(pidx // NZ, NX), pidx // (NZ * NX)
    loads = [
        pltpu.make_async_copy(src, dst, lsem.at[k])
        for k, (src, dst) in enumerate(((pm_h, pmap), (amp_h, amp), (lam_h, lam), (int_h, ints)))
    ]
    for load in loads[:3]:
        load.start()

    def at(yy, xx, zz):
        return ((yy * NX + xx) * NZ + zz, rep)

    def xs(d):
        return lax.rem(x + d, NX)

    def zs(d):
        return lax.rem(z + d, NZ)

    offsets = [(dy, dx) for dx in (2, 1, 3, 0) for dy in (1, 0) if (dy, dx) != (0, 0)]
    partners = [at(lax.rem(y + dy, NY), xs(dx), z) for dy, dx in offsets]
    partners += [at(y, x, zs(d)) for d in (1, NZ - 1)]
    core, ylo = lax.rem(rep, 2), rep // 2
    partners += [(pidx, 2 * ylo + 1 - core), (pidx, 2 * (1 - ylo) + core)]
    barrier = pltpu.get_barrier_semaphore()
    for device in partners:
        pl.semaphore_signal(barrier, inc=1, device_id=device, device_id_type=MESH)

    def greet(level):
        for d in (2**level, NZ - 2**level):
            pl.semaphore_signal(
                known.at[level], inc=1, device_id=at(y, x, zs(d)), device_id_type=MESH
            )

    count = [0]

    def send(blocks, into):
        k = count[0]
        count[0] += 1

        def copy_of(src, dst, device):
            return pltpu.make_async_remote_copy(
                src_ref=src, dst_ref=dst, send_sem=ssem.at[k], recv_sem=rsem.at[k],
                device_id=device, device_id_type=MESH,
            )

        for src, dst, device in blocks:
            copy_of(src, dst, device).start()
        return copy_of(into, into, blocks[0][2])

    rows = amp.shape[0]
    f32, bf16 = jnp.float32, jnp.bfloat16

    def iota(shape, dim):
        return lax.broadcasted_iota(jnp.int32, shape, dim)

    tiles = rows // TW
    kt, ntiles = pmap.shape
    loads[0].wait()
    sel = (iota((rows, ntiles), 1) == tiles * pidx + div3(iota((rows, ntiles), 0), 5)).astype(bf16)
    mask8 = lax.dot_general(
        sel, pmap[...].astype(bf16), (((1,), (1,)), ((), ())), preferred_element_type=f32
    ).astype(bf16)

    def mask_of(first, width):
        spread = (div3(first + iota((kt, width), 1), 5) == iota((kt, width), 0)).astype(bf16)
        return jnp.dot(mask8, spread, preferred_element_type=f32)

    kw = amp.shape[1]
    live_mask = mask_of(0, kw).astype(bf16)
    blk = 256
    eye = (iota((blk, 1), 0) == iota((blk, blk), 1)).astype(bf16)
    loads[1].wait()
    amp[...] = amp[...] * live_mask

    def turn(order, columns):
        return lax.dot_general(
            order, amp[:, columns], (((1,), (1,)), ((), ())), preferred_element_type=f32
        ).astype(bf16)

    for c0 in range(0, kw, blk):
        ampt[c0 : c0 + blk, :] = turn(eye, slice(c0, c0 + blk))
    loads[2].wait()
    loads[3].start()

    half = kw // 2
    zb = lax.rem(z, 2)
    mine = {"x": (x,), "y": (y,), "yx": (y, x), "p0": (zb,), "p1": (zb,)}
    peers = {
        "x": [((xs(k),), at(y, xs(k), z)) for k in (2, 1, 3)],
        "y": [((1 - y,), at(1 - y, x, z))],
        "yx": [
            ((lax.rem(y + dy, NY), xs(dx)), at(lax.rem(y + dy, NY), xs(dx), z)) for dy, dx in offsets
        ],
        "p0": [((1 - zb,), at(y, x, zs(NZ + 1 - 2 * zb)))],
        "p1": [((1 - zb,), at(y, x, zs(NZ - 1 + 2 * zb)))],
    }
    cur, recv, last, flying, flown = [], [], [], [], []
    for c0, width, steps in PARTS:
        cur.append([bufs.pop(0) for _ in steps])
        recv.append([bufs.pop(0) for _ in steps])
        last.append((bufs.pop(0), bufs.pop(0)))
        flying.append(None)

    def launch(n, s):
        into = recv[n][s]
        flying[n] = send(
            [
                (cur[n][s].at[block], into.at[k], device)
                for k, (block, device) in enumerate(peers[PARTS[n][2][s]])
            ],
            into,
        )

    def split_rows():
        quarter = kw // 4
        for hi in range(2):
            for lo in range(2):
                inner = iota((quarter, 1), 0)
                sixth = div3(inner, 1)
                source = 2 * OWN * sixth + OWN * hi + inner - OWN * sixth
                order = (source == iota((quarter, half), 1)).astype(bf16)
                r0 = hi * half + lo * quarter
                ampp[r0 : r0 + quarter, :] = turn(order, slice(lo * half, lo * half + half))

    split = False
    for n in START:
        c0, width, steps = PARTS[n]
        axes, deep, members = axes_of(steps)
        paired = deep < TW
        if paired and not split:
            split_rows()
            split = True
        for hi in range(2):
            block = jnp.dot(
                (ampp if paired else ampt)[hi * half : (hi + 1) * half, :], lam[:, c0 : c0 + width],
                preferred_element_type=f32,
            ).astype(bf16)
            for lo in range(half // deep):
                index = {"x": (lo % NX,), "p0": (hi,), "p1": (hi,)}
                index["y"] = (lo // NX if paired else hi,)
                index["yx"] = index["y"] + index["x"]
                where = sum((index[step] for step in steps), ())
                cur[n][0][where] = block[lo * deep : (lo + 1) * deep, :]
        if n == START[0]:
            pl.semaphore_wait(barrier, len(partners))
            greet(0)
        launch(n, 0)

    pl.semaphore_wait(known.at[0], 2)
    greet(1)
    loads[3].wait()
    wide = kw // NREP
    for r in range(NREP):
        part = lax.dot_general(
            lam[...], ints[r * wide : (r + 1) * wide, :], (((1,), (1,)), ((), ())),
            preferred_element_type=f32,
        )
        lpart[r % 2, r // 2] = (part * mask_of(r * wide, wide)).astype(bf16)
    over_core = send([(lpart.at[1 - core], lrecv, (pidx, 2 * ylo + 1 - core))], lrecv)
    pl.semaphore_wait(known.at[1], 2)
    greet(2)
    pl.semaphore_wait(known.at[2], 2)

    def spread_of(members):
        spread_rows = iota((members * PAD, 1), 0)
        slot = spread_rows & (PAD - 1)
        source = jnp.where(slot < OWN, (spread_rows >> 3) * OWN + slot, -1)
        return (source == iota((members * PAD, members * OWN), 1)).astype(bf16)

    def finish_step(n, s):
        c0, width, steps = PARTS[n]
        axes, deep, members = axes_of(steps)
        flying[n].wait_recv()
        flown.append(flying[n])
        total = cur[n][s][mine[steps[s]]].astype(f32)
        for k in range(recv[n][s].shape[0]):
            total += recv[n][s][k].astype(f32)
        if s + 1 < len(steps):
            cur[n][s + 1][...] = total.astype(bf16)
            launch(n, s + 1)
            return
        out, into = last[n]
        padded = jnp.dot(spread_of(members), total.astype(bf16), preferred_element_type=f32)
        out[...] = padded.reshape(members, PAD, width)[:, :OWN, :].astype(bf16)
        step = NZ // members
        place = z // step
        flying[n] = send(
            [
                (out.at[lax.rem(place + k, members)], into.at[k - 1], at(y, x, zs(k * step)))
                for k in sorted(range(1, members), key=lambda k: -min(k, members - k))
            ],
            into,
        )

    for k, (n, s) in enumerate(ORDER):
        if k == LAMBDA_AT[0]:
            over_core.wait()
            lsum[...] = (lpart[core].astype(f32) + lrecv[...].astype(f32)).astype(bf16)
        if k == LAMBDA_AT[1]:
            over_y = send([(lsum.at[1 - ylo], lfar, (pidx, 2 * (1 - ylo) + core))], lfar)
        finish_step(n, s)

    ncol = lam.shape[1]
    for c0 in range(0, ncol, 384):
        lad[:, c0 : c0 + 384] = jnp.dot(
            amp[...], ints[:, c0 : c0 + 384], preferred_element_type=f32
        ).astype(bf16)
    lad_copy = pltpu.make_async_copy(lad, lad_o, lsem.at[4])
    lad_copy.start()

    over_y.wait()
    for copies in flown:
        copies.wait_send()
    ll_o[...] = (lsum[ylo].astype(f32) + lfar[...].astype(f32)).astype(bf16)

    factor = 1.0 / (rows * NY * NX * NZ) ** 0.5
    for n in CLOSE:
        c0, width, steps = PARTS[n]
        out, into = last[n]
        members = out.shape[0]
        flying[n].wait()
        total = out[z // (NZ // members)].astype(f32)
        for k in range(members - 1):
            total += into[k].astype(f32)
        den_o[:, c0 : c0 + width] = total * factor
    lad_copy.wait()


def finish(lad_i, ll_i, den_i, lad_o, ll_o, den_o):
    lad_o[...] = lad_i[...]
    ll_o[...] = ll_i[...]
    den_o[...] = den_i[...]


def body(amplitudes, lambda_amps, integrals, pair_map):
    rows, kw = amplitudes.shape
    ncol = lambda_amps.shape[1]
    wide = kw // NREP
    bf16 = jnp.bfloat16
    scratch = [
        pltpu.VMEM((rows, kw), bf16),
        pltpu.VMEM((rows, ncol), bf16),
        pltpu.VMEM((kw, ncol), bf16),
        pltpu.VMEM(pair_map.shape[::-1], jnp.int32),
        pltpu.VMEM((kw, rows), bf16),
        pltpu.VMEM((kw, rows), bf16),
        pltpu.VMEM((rows, ncol), bf16),
        pltpu.VMEM((2, NREP // 2, rows, wide), bf16),
        pltpu.VMEM((NREP // 2, rows, wide), bf16),
        pltpu.VMEM((NREP // 2, rows, wide), bf16),
        pltpu.VMEM((rows, wide), bf16),
    ]
    sends = 2
    parts = []
    for _, width, steps in PARTS:
        axes, deep, members = axes_of(steps)
        dims = [sum(axes[s:], ()) + (deep,) for s in range(len(steps))]
        shapes = dims + [
            (math.prod(axes[s]) - 1,) + sum(axes[s + 1 :], ()) + (deep,) for s in range(len(steps))
        ]
        sends += len(steps) + 1
        shapes += [(members, OWN), (members - 1, OWN)]
        parts += [pltpu.VMEM(shape + (width,), bf16) for shape in shapes]
    scratch += [
        pltpu.SemaphoreType.DMA((5,)),
        pltpu.SemaphoreType.DMA((sends,)),
        pltpu.SemaphoreType.DMA((sends,)),
        pltpu.SemaphoreType.REGULAR((3,)),
    ]
    anywhere = pl.BlockSpec(memory_space=pl.ANY)
    vmem = pl.BlockSpec(memory_space=pltpu.VMEM)
    ladder, summed, density = pl.pallas_call(
        kernel,
        out_shape=(
            jax.ShapeDtypeStruct((rows, ncol), bf16),
            jax.ShapeDtypeStruct((rows, wide), bf16),
            jax.ShapeDtypeStruct((OWN, ncol), jnp.float32),
        ),
        in_specs=[anywhere] * 4,
        out_specs=(anywhere, vmem, vmem),
        scratch_shapes=scratch + parts,
        compiler_params=pltpu.CompilerParams(
            collective_id=0, has_side_effects=True, vmem_limit_bytes=56 * 2**20
        ),
        cost_estimate=pl.CostEstimate(
            flops=6 * rows * kw * ncol, bytes_accessed=4 * 2**20, transcendentals=0
        ),
    )(amplitudes, lambda_amps, integrals, pair_map.T)
    return pl.pallas_call(
        finish,
        out_shape=(
            jax.ShapeDtypeStruct((rows, ncol), bf16),
            jax.ShapeDtypeStruct((rows, wide), bf16),
            jax.ShapeDtypeStruct((OWN, ncol), jnp.float32),
        ),
        in_specs=[vmem] * 3,
        out_specs=(vmem,) * 3,
    )(ladder, summed, density)


def solution(mesh):
    in_specs = (P("pair", None), P("pair", "rep"), P(None, "rep"), P())
    out_specs = (P("pair", "rep"), P("pair", "rep"), P("pair", "rep"))
    return jax.shard_map(body, mesh=mesh, in_specs=in_specs, out_specs=out_specs, check_vma=False)
```
